256 devices in a mesh: group: 8 (over y, core), rows: 32 (over z, x).
Axes of the slice: x: 4, y: 4, z: 8, core: 2. Of those that a mesh axis runs over, the one named last changes fastest.
Arguments:
- features: bfloat16 [131072, 8192], P(('group', 'rows')), may hold values from -6 to 6
- labels: int32 [131072], P(('group', 'rows')), may hold values from 0 to 15
- weights: float32 [16, 8192], replicated, may hold values from -0.0625 to 0.0625
Outputs:
- new_logits: float32 [16, 131072], P(None, ('group', 'rows'))
The draws below stay inside these ranges and needn't reach their ends.
All inputs are finite; a program needn't handle non-finite values.
Results may differ from the reference program's by a relative error of at most 0.0048.
Values may be sent and summed in bfloat16 or wider, within the bound.
A program may use at most 64 MiB of HBM per device.

```python
import jax
import jax.numpy as jnp
from jax import lax

D = 8192
K = 16
ITERS = 2
ROWS_ALL = 131072
N_GROUP = 8


def touch_ends(result, stream_key, smallest, largest):
    extent = result.shape
    spot = [jax.random.randint(jax.random.fold_in(stream_key, axis), (), 0, extent[axis]) for axis in range(len(extent))]
    result = result.at[tuple(spot)].set(smallest)
    longest = extent.index(max(extent))
    spot[longest] = (spot[longest] + 1) % extent[longest]
    return result.at[tuple(spot)].set(largest)


def levels(own_key, dims, shards, least, largest):
    gain, own = 1.0, jax.random.fold_in(own_key, 6)
    for axis_at, blocks in shards:
        steps = jnp.exp(jax.random.uniform(jax.random.fold_in(own, axis_at), (blocks,), jnp.float32, least / len(shards), largest / len(shards)))
        gain = gain * jnp.repeat(steps, dims[axis_at] // blocks).reshape([-1 if axis == axis_at else 1 for axis in range(len(dims))])
    return gain


def scatter_about(stream_key, extent, spread, limit, cuts=(), held_as=jnp.bfloat16):
    array = jax.random.normal(stream_key, extent, jnp.float32) * spread
    if len(cuts) > 0:
        array = levels(stream_key, extent, cuts, -0.22, 0.18) * array
    return jnp.clip(array, min=-limit, max=limit).astype(held_as)


def setup_inputs(seed: int = 0) -> dict:
    key_of = jax.random.split(jax.random.key(seed), 4)
    return {
        "features": scatter_about(key_of[0], (ROWS_ALL, D), 1.0, 6.0, ((0, 256),)),
        "labels": touch_ends(jax.random.randint(key_of[1], (ROWS_ALL,), 0, K), jax.random.fold_in(key_of[1], 1), 0, K - 1).astype(jnp.int32),
        "weights": scatter_about(key_of[2], (K, D), D ** -0.5, 0.0625, (), jnp.float32),
    }


ridge = 0.001


def rows_product(left, data):
    return lax.dot_general(left, data, (((1,), (1,)), ((), ())), preferred_element_type=jnp.float32)


def reference(features, labels, weights):
    total = features.shape[0]
    logits = rows_product(weights.astype(jnp.bfloat16), features)
    prob = jax.nn.softmax(logits, axis=0)
    onehot = (labels[None, :] == jnp.arange(K, dtype=jnp.int32)[:, None]).astype(jnp.float32)
    resid = (prob - onehot).astype(jnp.bfloat16)
    grad = jnp.dot(resid, features, preferred_element_type=jnp.float32) / total + ridge * weights
    shard_rows = total // N_GROUP

    def solve(index):
        start = (index * shard_rows).astype(jnp.int32)
        local = lax.dynamic_slice_in_dim(features, start, shard_rows, 0)
        local_prob = lax.dynamic_slice_in_dim(prob, start, shard_rows, 1)

        def hessian(vector):
            inner = rows_product(vector.astype(jnp.bfloat16), local)
            weighted = local_prob * (inner - jnp.sum(local_prob * inner, axis=0, keepdims=True))
            term = jnp.dot(weighted.astype(jnp.bfloat16), local, preferred_element_type=jnp.float32)
            return term / shard_rows + ridge * vector

        answer = jnp.zeros_like(grad)
        residual = -grad
        search = residual
        norm_now = jnp.sum(residual * residual)
        for step in range(ITERS):
            image = hessian(search)
            alpha = norm_now / jnp.sum(search * image)
            answer = answer + alpha * search
            residual = residual - alpha * image
            norm_next = jnp.sum(residual * residual)
            search = residual + (norm_next / norm_now) * search
            norm_now = norm_next
        return answer

    directions = lax.map(solve, jnp.arange(N_GROUP, dtype=jnp.int32))
    step_mean = jnp.sum(directions, axis=0) / N_GROUP
    return logits + rows_product(step_mean.astype(jnp.bfloat16), features)
```

```python
import functools

import jax
import jax.numpy as jnp
from jax import lax
from jax.experimental import pallas as pl
from jax.experimental.pallas import tpu as pltpu
from jax.sharding import PartitionSpec as P

RIDGE = 0.001
MESH = pl.DeviceIdType.MESH
NT = (((1,), (1,)), ((), ()))
F32 = jnp.float32
BF16 = jnp.bfloat16


def rows_product(left, data):
    return lax.dot_general(left, data, NT, preferred_element_type=F32)


def total_of(array):
    return jnp.sum(jnp.sum(array, axis=0, keepdims=True), axis=1, keepdims=True)


def kernel(
    dims,
    labels_ref,
    w_hbm,
    f_hbm,
    out_ref,
    feat,
    wts,
    part,
    got,
    line_src,
    line,
    first,
    term,
    gotx,
    zsrc,
    gotz,
    sums,
    stat_src,
    stat_z,
    stat_y,
    load_sem,
    w_sem,
    send,
    recv,
    first_sem,
    agx_sem,
    bulk_sem,
    fwd_sem,
):
    ny, nz, nx = dims
    ng = 2 * ny
    classes, depth = wts.shape
    rows = feat.shape[0]
    slices = ng * nx
    wide = depth // slices
    block = depth // ng
    xblock = depth // nx
    zwide = xblock // nz
    shard_rows = rows * nz * nx
    total_rows = shard_rows * ng

    g, r = lax.axis_index("group"), lax.axis_index("rows")
    y, c = g // 2, g % 2
    z, x = r // nx, r % nx
    mine = g * nx + x

    def cols(start, size):
        return pl.ds(pl.multiple_of(start, 128), size)

    def push(src, dst, ssem, rsem, gg, zz, xx):
        pltpu.make_async_remote_copy(
            src_ref=src,
            dst_ref=dst,
            send_sem=ssem,
            recv_sem=rsem,
            device_id=(gg, zz * nx + xx),
            device_id_type=MESH,
        ).start()

    def wait(ref, sem):
        pltpu.make_async_copy(ref, ref, sem).wait()

    w_copy = pltpu.make_async_copy(w_hbm, wts, w_sem)
    w_copy.start()
    loads = []
    for k in range(ng):
        span = pl.ds(k * block, block)
        loads.append(pltpu.make_async_copy(f_hbm.at[:, span], feat.at[:, span], load_sem.at[k]))
        loads[-1].start()
    barrier = pltpu.get_barrier_semaphore()

    def greet(k, carry):
        j = (mine + k) % slices
        pl.semaphore_signal(barrier, 1, device_id=(j // nx, z * nx + j % nx), device_id_type=MESH)
        return carry

    lax.fori_loop(1, slices, greet, 0)
    for k in range(1, nz):
        pl.semaphore_signal(barrier, 1, device_id=(g, ((z + k) % nz) * nx + x), device_id_type=MESH)

    w_copy.wait()
    logits = jnp.zeros((classes, rows), F32)
    for k in range(ng):
        loads[k].wait()
        span = slice(k * block, (k + 1) * block)
        logits += rows_product(wts[:, span].astype(BF16), feat[:, span])
    e = jnp.exp(logits - jnp.max(logits, axis=0, keepdims=True))
    prob = e / jnp.sum(e, axis=0, keepdims=True)
    onehot = labels_ref[...] == lax.broadcasted_iota(jnp.int32, (classes, rows), 0)
    resid = (prob - onehot.astype(F32)).astype(BF16)

    pl.semaphore_wait(barrier, slices - 1 + nz - 1)
    for k in list(range(1, ng)) + [0]:
        gg = (g + k) % ng
        span = cols(gg * block, block)
        part[:, span] = jnp.dot(resid, feat[:, span], preferred_element_type=F32).astype(BF16)
        for i in range(nx):
            if k == 0 and i == 0:
                continue
            xx = (x + i) % nx
            push(part.at[:, cols(gg * block + xx * wide, wide)], got.at[mine], send.at[0], recv.at[0], gg, z, xx)
    got[mine] = part[:, cols(mine * wide, wide)]
    wait(got.at[pl.ds(0, slices - 1)], recv.at[0])
    share = jnp.zeros((classes, wide), F32)
    for k in range(slices):
        share += got[k].astype(F32)
    line_src[...] = share.astype(BF16)
    for k in range(1, nz):
        push(line_src, line.at[z], send.at[1], recv.at[1], g, (z + k) % nz, x)
    line[z] = line_src[...]
    wait(line.at[pl.ds(0, nz - 1)], recv.at[1])
    share = jnp.zeros((classes, wide), F32)
    for k in range(nz):
        share += line[k].astype(F32)
    own = cols(mine * wide, wide)
    first[:, own] = (-(share / total_rows + RIDGE * wts[:, own])).astype(BF16)

    def spread(k, carry):
        j = (mine + k) % slices
        push(first.at[:, own], first.at[:, own], send.at[2], first_sem.at[g], j // nx, z, j % nx)
        return carry

    lax.fori_loop(1, slices, spread, 0)

    u1 = jnp.zeros((classes, rows), F32)
    for k in range(ng):
        gg = (g + k) % ng
        span = cols(gg * block, block)
        if k == 0:
            wait(got.at[pl.ds(0, nx - 1)], first_sem.at[gg])
        else:
            wait(first.at[:, span], first_sem.at[gg])
        u1 += rows_product(first[:, span], feat[:, span])
    c1 = (prob * (u1 - jnp.sum(prob * u1, axis=0, keepdims=True))).astype(BF16)

    for k in list(range(1, nx)) + [0]:
        xx = (x + k) % nx
        span = cols(xx * xblock, xblock)
        term[:, span] = jnp.dot(c1, feat[:, span], preferred_element_type=F32).astype(BF16)
        if k:
            push(term.at[:, span], gotx.at[x], send.at[3], recv.at[3], g, z, xx)
    gotx[x] = term[:, cols(x * xblock, xblock)]
    rr0 = jnp.zeros((1, 1), F32)
    for k in range(ng):
        r0 = first[:, k * block : (k + 1) * block].astype(F32)
        rr0 += total_of(r0 * r0)
    wait(gotx.at[pl.ds(0, nx - 1)], recv.at[3])
    for k in range(nz):
        span = slice(k * zwide, (k + 1) * zwide)
        share = jnp.zeros((classes, zwide), F32)
        for i in range(nx):
            share += gotx[i, :, span].astype(F32)
        zsrc[k] = share.astype(BF16)
    for k in range(1, nz):
        zz = (z + k) % nz
        push(zsrc.at[zz], gotz.at[z], send.at[4], recv.at[4], g, zz, x)
    gotz[z] = zsrc[z]
    wait(gotz.at[pl.ds(0, nz - 1)], recv.at[4])
    share = jnp.zeros((classes, zwide), F32)
    for k in range(nz):
        share += gotz[k].astype(F32)

    slot = c * ny + y
    own = cols(x * xblock + z * zwide, zwide)
    sums[slot, :, own] = share.astype(BF16)
    for k in range(1, nz):
        push(sums.at[slot, :, own], sums.at[slot, :, own], send.at[5], recv.at[5], g, (z + k) % nz, x)
    wait(gotz.at[pl.ds(0, nz - 1)], recv.at[5])

    def on_to_others(span):
        for k in range(1, ny):
            yy = (y + k) % ny
            push(sums.at[slot, :, span], sums.at[slot, :, span], send.at[7], bulk_sem.at[y], yy * 2 + c, z, x)
        push(sums.at[slot, :, span], sums.at[slot, :, span], send.at[8], fwd_sem.at[y], y * 2 + 1 - c, z, x)

    own = cols(x * xblock, xblock)
    for k in range(1, nx):
        push(sums.at[slot, :, own], sums.at[slot, :, own], send.at[6], agx_sem.at[x], g, z, (x + k) % nx)
    on_to_others(own)
    w1 = rows_product(sums[slot, :, own], feat[:, own])
    for k in (1, nx - 1, *range(2, nx - 1)) if nx > 2 else (1,):
        xx = (x + k) % nx
        span = cols(xx * xblock, xblock)
        wait(sums.at[slot, :, span], agx_sem.at[xx])
        on_to_others(span)
        w1 += rows_product(sums[slot, :, span], feat[:, span])

    r0_hp = jnp.zeros((1, 1), F32)
    for k in range(ng):
        span = slice(k * block, (k + 1) * block)
        r0 = first[:, span].astype(F32)
        hp = sums[slot, :, span].astype(F32) / shard_rows + RIDGE * r0
        r0_hp += total_of(r0 * hp)
    alpha1 = rr0 / r0_hp
    rr1 = jnp.zeros((1, 1), F32)
    for k in range(ng):
        span = slice(k * block, (k + 1) * block)
        r0 = first[:, span].astype(F32)
        hp = sums[slot, :, span].astype(F32) / shard_rows + RIDGE * r0
        r1 = r0 - alpha1 * hp
        rr1 += total_of(r1 * r1)
    beta = rr1 / rr0
    pp = jnp.zeros((1, 1), F32)
    for k in range(ng):
        span = slice(k * block, (k + 1) * block)
        r0 = first[:, span].astype(F32)
        hp = sums[slot, :, span].astype(F32) / shard_rows + RIDGE * r0
        p2 = r0 - alpha1 * hp + beta * r0
        pp += total_of(p2 * p2)
    u2 = u1 + beta * u1 - alpha1 * (w1 / shard_rows + RIDGE * u1)
    c2 = (prob * (u2 - jnp.sum(prob * u2, axis=0, keepdims=True))).astype(BF16).astype(F32)
    curve = total_of(c2 * u2)

    row = lax.broadcasted_iota(jnp.int32, (8, 128), 0)
    rest = jnp.where(row == 1, rr1, jnp.where(row == 2, pp, jnp.where(row == 3, alpha1, beta)))
    stat_src[0] = jnp.where(row == 0, curve, rest)
    for k in range(1, nz):
        push(stat_src.at[0], stat_z.at[z], send.at[9], recv.at[6], g, (z + k) % nz, x)
    stat_z[z] = stat_src[0]
    wait(stat_z.at[pl.ds(0, nz - 1)], recv.at[6])
    curve = jnp.zeros((8, 128), F32)
    for k in range(nz):
        curve += stat_z[k]
    stat_src[1] = jnp.where(row == 0, curve, rest)

    def tell(k, carry):
        j = (mine + k) % slices
        push(stat_src.at[1], stat_y.at[mine], send.at[10], recv.at[7], j // nx, z, j % nx)
        return carry

    lax.fori_loop(1, slices, tell, 0)
    stat_y[mine] = stat_src[1]

    for k in range(1, ny):
        yy = (y + k) % ny
        there = sums.at[c * ny + yy]
        wait(there, bulk_sem.at[yy])
        push(there, there, send.at[11], fwd_sem.at[yy], y * 2 + 1 - c, z, x)
    for k in range(ny):
        wait(sums.at[(1 - c) * ny + k], fwd_sem.at[k])
    w_all = jnp.zeros((ng * classes, rows), F32)
    for k in range(ng):
        span = slice(k * block, (k + 1) * block)
        w_all += rows_product(sums[:, :, span].reshape(ng * classes, block), feat[:, span])

    wait(stat_y.at[pl.ds(0, slices - 1)], recv.at[7])
    scale = jnp.zeros((1, 1), F32)
    result = logits
    for core in range(2):
        for yy in range(ny):
            at = (yy * 2 + core) * nx
            stats = stat_y[at]
            for i in range(1, nx):
                stats = jnp.where(row == 0, stats + stat_y[at + i], stats)
            curve, rr, pp, alpha, beta = (stats[i : i + 1, 0:1] for i in range(5))
            alpha2 = rr / (curve / shard_rows + RIDGE * pp)
            scale += alpha + alpha2 * (1.0 + beta - RIDGE * alpha)
            there = (core * ny + yy) * classes
            result -= (alpha * alpha2 / (ng * shard_rows)) * w_all[there : there + classes]
    out_ref[...] = result + (scale / ng) * u1

    wait(got.at[pl.ds(0, slices - 1)], send.at[0])
    wait(line.at[pl.ds(0, nz - 1)], send.at[1])
    wait(got.at[pl.ds(0, slices - 1)], send.at[2])
    wait(gotx.at[pl.ds(0, nx - 1)], send.at[3])
    wait(gotz.at[pl.ds(0, nz - 1)], send.at[4])
    wait(gotz.at[pl.ds(0, nz - 1)], send.at[5])
    wait(gotx.at[pl.ds(0, nx - 1)], send.at[6])
    wait(sums.at[pl.ds(0, ny - 1)], send.at[7])
    wait(sums.at[0], send.at[8])
    wait(stat_z.at[pl.ds(0, nz - 1)], send.at[9])
    wait(stat_y.at[pl.ds(0, slices - 1)], send.at[10])
    wait(sums.at[pl.ds(0, ny - 1)], send.at[11])


def per_device(dims, features, labels, weights):
    ny, nz, nx = dims
    ng = 2 * ny
    rows, depth = features.shape
    classes = weights.shape[0]
    slices = ng * nx
    wide, xblock = depth // slices, depth // nx
    zwide = xblock // nz
    dma = pltpu.SemaphoreType.DMA
    return pl.pallas_call(
        functools.partial(kernel, dims),
        out_shape=jax.ShapeDtypeStruct((classes, rows), F32),
        in_specs=[
            pl.BlockSpec(memory_space=pltpu.VMEM),
            pl.BlockSpec(memory_space=pl.ANY),
            pl.BlockSpec(memory_space=pl.ANY),
        ],
        out_specs=pl.BlockSpec(memory_space=pltpu.VMEM),
        scratch_shapes=[
            pltpu.VMEM((rows, depth), BF16),
            pltpu.VMEM((classes, depth), F32),
            pltpu.VMEM((classes, depth), BF16),
            pltpu.VMEM((slices, classes, wide), BF16),
            pltpu.VMEM((classes, wide), BF16),
            pltpu.VMEM((nz, classes, wide), BF16),
            pltpu.VMEM((classes, depth), BF16),
            pltpu.VMEM((classes, depth), BF16),
            pltpu.VMEM((nx, classes, xblock), BF16),
            pltpu.VMEM((nz, classes, zwide), BF16),
            pltpu.VMEM((nz, classes, zwide), BF16),
            pltpu.VMEM((ng, classes, depth), BF16),
            pltpu.VMEM((2, 8, 128), F32),
            pltpu.VMEM((nz, 8, 128), F32),
            pltpu.VMEM((slices, 8, 128), F32),
            dma((ng,)),
            dma,
            dma((12,)),
            dma((8,)),
            dma((ng,)),
            dma((nx,)),
            dma((ny,)),
            dma((ny,)),
        ],
        compiler_params=pltpu.CompilerParams(
            vmem_limit_bytes=40 * 2**20, collective_id=0, has_side_effects=True
        ),
        name="newton_step",
    )(labels.reshape(1, rows), weights, features)


def solution(mesh, nx=4):
    dims = (mesh.shape["group"] // 2, mesh.shape["rows"] // nx, nx)
    return jax.shard_map(
        functools.partial(per_device, dims),
        mesh=mesh,
        in_specs=(P(("group", "rows"), None), P(("group", "rows")), P()),
        out_specs=P(None, ("group", "rows")),
        check_vma=False,
    )
```

```python
import functools

import jax
import jax.numpy as jnp
from jax import lax
from jax.experimental import pallas as pl
from jax.experimental.pallas import tpu as pltpu
from jax.sharding import PartitionSpec as P

RIDGE = 0.001
MESH = pl.DeviceIdType.MESH
NT = (((1,), (1,)), ((), ()))
F32 = jnp.float32
BF16 = jnp.bfloat16


def rows_product(left, data):
    return lax.dot_general(left, data, NT, preferred_element_type=F32)


def total_of(array):
    return jnp.sum(jnp.sum(array, axis=0, keepdims=True), axis=1, keepdims=True)


def near(n):
    return sorted(range(n), key=lambda k: min(k, n - k))


def kernel(
    dims,
    labels_hbm,
    w_hbm,
    f_hbm,
    out_ref,
    feat,
    labels,
    wts,
    pair_src,
    pair,
    part,
    got,
    line_src,
    line,
    first,
    term,
    gotx,
    zsrc,
    gotz,
    sums,
    stat_src,
    stat_z,
    stat_y,
    load_sem,
    w_sem,
    label_sem,
    send,
    recv,
    pair_sem,
    first_sem,
    cross_sem,
    rsx_sem,
    agz_sem,
    agx_sem,
    bulk_sem,
    fwd_sem,
):
    ny, nz, nx = dims
    ng = 2 * ny
    classes, depth = wts.shape
    rows = feat.shape[0]
    plane = ny * nx
    half = depth // 2
    block = half // ny
    wide = block // nx
    zblock = depth // nz
    zwide = zblock // nx
    shard_rows = rows * nz * nx
    total_rows = shard_rows * ng
    near_y, near_z, near_x = near(ny), near(nz), near(nx)

    g, r = lax.axis_index("group"), lax.axis_index("rows")
    y, c = g // 2, g % 2
    z, x = r // nx, r % nx
    slot = c * ny + y

    def cols(start, size):
        return pl.ds(pl.multiple_of(start, 128), size)

    def push(src, dst, ssem, rsem, yy, cc, zz, xx):
        pltpu.make_async_remote_copy(
            src_ref=src,
            dst_ref=dst,
            send_sem=ssem,
            recv_sem=rsem,
            device_id=(yy * 2 + cc, zz * nx + xx),
            device_id_type=MESH,
        ).start()

    def wait(ref, sem):
        pltpu.make_async_copy(ref, ref, sem).wait()

    w_copy = pltpu.make_async_copy(w_hbm, wts, w_sem)
    w_copy.start()
    label_copy = pltpu.make_async_copy(labels_hbm, labels, label_sem)
    label_copy.start()
    loads = []
    for k in range(ng):
        span = pl.ds(k * (depth // ng), depth // ng)
        loads.append(pltpu.make_async_copy(f_hbm.at[:, span], feat.at[:, span], load_sem.at[k]))
        loads[-1].start()
    barrier = pltpu.get_barrier_semaphore()
    others = [(j, k, i) for j in near_y[::-1] for k in near_x[::-1] for i in (1, 0) if (j, k, i) != (0, 0, 0)]
    others.sort(key=lambda o: -min(o[0], ny - o[0]) - min(o[1], nx - o[1]))
    for j, k, i in others:
        there = (((y + j) % ny) * 2 + (c + i) % 2, z * nx + (x + k) % nx)
        pl.semaphore_signal(barrier, 1, device_id=there, device_id_type=MESH)
    for k in near_z[:0:-1]:
        pl.semaphore_signal(barrier, 1, device_id=(g, ((z + k) % nz) * nx + x), device_id_type=MESH)

    w_copy.wait()
    logits = jnp.zeros((classes, rows), F32)
    for k in range(ng):
        loads[k].wait()
        span = slice(k * (depth // ng), (k + 1) * (depth // ng))
        logits += rows_product(wts[:, span].astype(BF16), feat[:, span])
    e = jnp.exp(logits - jnp.max(logits, axis=0, keepdims=True))
    prob = e / jnp.sum(e, axis=0, keepdims=True)
    label_copy.wait()
    onehot = labels[...] == lax.broadcasted_iota(jnp.int32, (classes, rows), 0)
    resid = (prob - onehot.astype(F32)).astype(BF16)

    pl.semaphore_wait(barrier, len(others) + nz - 1)
    for j in near_y[::-1]:
        yy = (y + j) % ny
        span = cols((1 - c) * half + yy * block, block)
        pair_src[yy] = jnp.dot(resid, feat[:, span], preferred_element_type=F32)
        push(pair_src.at[yy], pair.at[yy], send.at[0], pair_sem.at[yy], y, 1 - c, z, x)
    for j in near_y[::-1]:
        yy = (y + j) % ny
        begin = c * half + yy * block
        mine = jnp.dot(resid, feat[:, cols(begin, block)], preferred_element_type=F32)
        wait(pair.at[yy], pair_sem.at[yy])
        part[:, cols(begin, block)] = (mine + pair[yy]).astype(BF16)
        for k in near_x[::-1]:
            xx = (x + k) % nx
            if j or k:
                there = part.at[:, cols(begin + xx * wide, wide)]
                push(there, got.at[y * nx + x], send.at[1], recv.at[0], yy, c, z, xx)
    own = cols(slot * block + x * wide, wide)
    got[y * nx + x] = part[:, own]
    wait(got.at[pl.ds(0, plane - 1)], recv.at[0])
    share = jnp.zeros((classes, wide), F32)
    for k in range(plane):
        share += got[k].astype(F32)
    line_src[...] = share
    for k in near_z[:0:-1]:
        push(line_src, line.at[z], send.at[2], recv.at[1], y, c, (z + k) % nz, x)
    line[z] = line_src[...]
    wait(line.at[pl.ds(0, nz - 1)], recv.at[1])
    share = jnp.zeros((classes, wide), F32)
    for k in range(nz):
        share += line[k]
    first[:, own] = (-(share / total_rows + RIDGE * wts[:, own])).astype(BF16)
    for j, k, i in others:
        if i == 0:
            push(first.at[:, own], first.at[:, own], send.at[3], first_sem.at[y], (y + j) % ny, c, z, (x + k) % nx)

    u1 = jnp.zeros((classes, rows), F32)
    for j in near_y:
        yy = (y + j) % ny
        span = cols(c * half + yy * block, block)
        wait(got.at[pl.ds(0, nx if j else nx - 1)], first_sem.at[yy])
        push(first.at[:, span], first.at[:, span], send.at[4], cross_sem.at[yy], y, 1 - c, z, x)
        u1 += rows_product(first[:, span], feat[:, span])
    for j in near_y:
        yy = (y + j) % ny
        span = cols((1 - c) * half + yy * block, block)
        wait(first.at[:, span], cross_sem.at[yy])
        u1 += rows_product(first[:, span], feat[:, span])
    c1 = (prob * (u1 - jnp.sum(prob * u1, axis=0, keepdims=True))).astype(BF16)

    for k in near_z[::-1]:
        zz = (z + k) % nz
        begin = zz * zblock
        term[:, cols(begin, zblock)] = jnp.dot(
            c1, feat[:, cols(begin, zblock)], preferred_element_type=F32
        ).astype(BF16)
        for i in near_x[:0:-1]:
            xx = (x + i) % nx
            push(term.at[:, cols(begin + xx * zwide, zwide)], gotx.at[zz, x], send.at[5], rsx_sem.at[zz], y, c, z, xx)
        gotx[zz, x] = term[:, cols(begin + x * zwide, zwide)]
    rr0 = jnp.zeros((1, 1), F32)
    for k in range(ng):
        r0 = first[:, k * block : (k + 1) * block].astype(F32)
        rr0 += total_of(r0 * r0)
    for k in near_z[::-1]:
        zz = (z + k) % nz
        wait(gotx.at[zz, pl.ds(0, nx - 1)], rsx_sem.at[zz])
        share = jnp.zeros((classes, zwide), F32)
        for i in range(nx):
            share += gotx[zz, i].astype(F32)
        if k:
            zsrc[zz] = share.astype(BF16)
            push(zsrc.at[zz], gotz.at[z], send.at[6], recv.at[2], y, c, zz, x)
        else:
            gotz[z] = share.astype(BF16)
    wait(gotz.at[pl.ds(0, nz - 1)], recv.at[2])
    share = jnp.zeros((classes, zwide), F32)
    for k in range(nz):
        share += gotz[k].astype(F32)

    own = cols(z * zblock + x * zwide, zwide)
    sums[slot, :, own] = share.astype(BF16)
    for k in near_z[:0:-1]:
        push(sums.at[slot, :, own], sums.at[slot, :, own], send.at[7], agz_sem.at[z], y, c, (z + k) % nz, x)
    for k in near_z:
        zz = (z + k) % nz
        span = cols(zz * zblock + x * zwide, zwide)
        if k:
            wait(sums.at[slot, :, span], agz_sem.at[zz])
        for i in near_x[:0:-1]:
            push(sums.at[slot, :, span], sums.at[slot, :, span], send.at[8], agx_sem.at[zz], y, c, z, (x + i) % nx)

    w1 = jnp.zeros((classes, rows), F32)
    for n, k in enumerate(near_z):
        zz = (z + k) % nz
        span = cols(zz * zblock, zblock)
        wait(gotx.at[0, pl.ds(0, nx - 1)], agx_sem.at[zz])
        for j in near_y[:0:-1]:
            there = sums.at[slot, :, span]
            push(there, there, send.at[9], bulk_sem.at[y, n // (nz // 2)], (y + j) % ny, c, z, x)
        w1 += rows_product(sums[slot, :, span], feat[:, span])

    r0_hp = jnp.zeros((1, 1), F32)
    for k in range(ng):
        span = slice(k * block, (k + 1) * block)
        r0 = first[:, span].astype(F32)
        hp = sums[slot, :, span].astype(F32) / shard_rows + RIDGE * r0
        r0_hp += total_of(r0 * hp)
    alpha1 = rr0 / r0_hp
    rr1 = jnp.zeros((1, 1), F32)
    for k in range(ng):
        span = slice(k * block, (k + 1) * block)
        r0 = first[:, span].astype(F32)
        hp = sums[slot, :, span].astype(F32) / shard_rows + RIDGE * r0
        r1 = r0 - alpha1 * hp
        rr1 += total_of(r1 * r1)
    beta = rr1 / rr0
    pp = jnp.zeros((1, 1), F32)
    for k in range(ng):
        span = slice(k * block, (k + 1) * block)
        r0 = first[:, span].astype(F32)
        hp = sums[slot, :, span].astype(F32) / shard_rows + RIDGE * r0
        p2 = r0 - alpha1 * hp + beta * r0
        pp += total_of(p2 * p2)
    u2 = u1 + beta * u1 - alpha1 * (w1 / shard_rows + RIDGE * u1)
    c2 = (prob * (u2 - jnp.sum(prob * u2, axis=0, keepdims=True))).astype(BF16).astype(F32)
    curve = total_of(c2 * u2)

    row = lax.broadcasted_iota(jnp.int32, (8, 128), 0)
    rest = jnp.where(row == 1, rr1, jnp.where(row == 2, pp, jnp.where(row == 3, alpha1, beta)))
    stat_src[0] = jnp.where(row == 0, curve, rest)
    for k in near_z[:0:-1]:
        push(stat_src.at[0], stat_z.at[z], send.at[10], recv.at[3], y, c, (z + k) % nz, x)
    stat_z[z] = stat_src[0]
    push(sums.at[slot], sums.at[slot], send.at[11], recv.at[4], y, 1 - c, z, x)

    def pass_on(n):
        for j in near_y[1:]:
            yy = (y + j) % ny
            wait(sums.at[0, :, pl.ds(0, half)], bulk_sem.at[yy, n])
            for k in near_z[n * (nz // 2) : (n + 1) * (nz // 2)]:
                there = sums.at[c * ny + yy, :, cols(((z + k) % nz) * zblock, zblock)]
                push(there, there, send.at[12], fwd_sem.at[yy, n], y, 1 - c, z, x)

    def products(n):
        for j in near_y[1:]:
            wait(sums.at[0, :, pl.ds(0, half)], fwd_sem.at[(y + j) % ny, n])
        total = jnp.zeros((ng * classes, rows), F32)
        for k in near_z[n * (nz // 2) : (n + 1) * (nz // 2)]:
            span = cols(((z + k) % nz) * zblock, zblock)
            total += rows_product(sums[:, :, span].reshape(ng * classes, zblock), feat[:, span])
        return total

    pass_on(0)
    wait(stat_z.at[pl.ds(0, nz - 1)], recv.at[3])
    curve = jnp.zeros((8, 128), F32)
    for k in range(nz):
        curve += stat_z[k]
    stat_src[1] = jnp.where(row == 0, curve, rest)
    for j, k, i in others:
        push(
            stat_src.at[1], stat_y.at[slot * nx + x], send.at[13], recv.at[5],
            (y + j) % ny, (c + i) % 2, z, (x + k) % nx,
        )
    stat_y[slot * nx + x] = stat_src[1]
    wait(sums.at[0], recv.at[4])
    w_all = products(0)
    pass_on(1)
    w_all += products(1)

    wait(stat_y.at[pl.ds(0, ng * nx - 1)], recv.at[5])
    scale = jnp.zeros((1, 1), F32)
    result = logits
    for there in range(ng):
        stats = stat_y[there * nx]
        for i in range(1, nx):
            stats = jnp.where(row == 0, stats + stat_y[there * nx + i], stats)
        curve, rr, pp, alpha, beta = (stats[i : i + 1, 0:1] for i in range(5))
        alpha2 = rr / (curve / shard_rows + RIDGE * pp)
        scale += alpha + alpha2 * (1.0 + beta - RIDGE * alpha)
        result -= (alpha * alpha2 / (ng * shard_rows)) * w_all[there * classes : (there + 1) * classes]
    out_ref[...] = result + (scale / ng) * u1

    wait(pair_src, send.at[0])
    wait(got.at[pl.ds(0, plane - 1)], send.at[1])
    wait(line.at[pl.ds(0, nz - 1)], send.at[2])
    wait(got.at[pl.ds(0, plane - 1)], send.at[3])
    wait(first.at[:, pl.ds(0, half)], send.at[4])
    wait(gotx.at[:, pl.ds(0, nx - 1)], send.at[5])
    wait(gotz.at[pl.ds(0, nz - 1)], send.at[6])
    wait(gotz.at[pl.ds(0, nz - 1)], send.at[7])
    wait(gotx.at[:, pl.ds(0, nx - 1)], send.at[8])
    wait(sums.at[pl.ds(0, ny - 1)], send.at[9])
    wait(stat_z.at[pl.ds(0, nz - 1)], send.at[10])
    wait(sums.at[0], send.at[11])
    wait(sums.at[pl.ds(0, ny - 1)], send.at[12])
    wait(stat_y.at[pl.ds(0, ng * nx - 1)], send.at[13])


def per_device(dims, features, labels, weights):
    ny, nz, nx = dims
    ng = 2 * ny
    rows, depth = features.shape
    classes = weights.shape[0]
    block = depth // ng
    wide, zwide = block // nx, depth // (nz * nx)
    dma = pltpu.SemaphoreType.DMA
    any_space = pl.BlockSpec(memory_space=pl.ANY)
    return pl.pallas_call(
        functools.partial(kernel, dims),
        out_shape=jax.ShapeDtypeStruct((classes, rows), F32),
        in_specs=[any_space] * 3,
        out_specs=pl.BlockSpec(memory_space=pltpu.VMEM),
        scratch_shapes=[
            pltpu.VMEM((rows, depth), BF16),
            pltpu.VMEM((1, rows), jnp.int32),
            pltpu.VMEM((classes, depth), F32),
            pltpu.VMEM((ny, classes, block), F32),
            pltpu.VMEM((ny, classes, block), F32),
            pltpu.VMEM((classes, depth), BF16),
            pltpu.VMEM((ny * nx, classes, wide), BF16),
            pltpu.VMEM((classes, wide), F32),
            pltpu.VMEM((nz, classes, wide), F32),
            pltpu.VMEM((classes, depth), BF16),
            pltpu.VMEM((classes, depth), BF16),
            pltpu.VMEM((nz, nx, classes, zwide), BF16),
            pltpu.VMEM((nz, classes, zwide), BF16),
            pltpu.VMEM((nz, classes, zwide), BF16),
            pltpu.VMEM((ng, classes, depth), BF16),
            pltpu.VMEM((2, 8, 128), F32),
            pltpu.VMEM((nz, 8, 128), F32),
            pltpu.VMEM((ng * nx, 8, 128), F32),
            dma((ng,)),
            dma,
            dma,
            dma((14,)),
            dma((6,)),
            dma((ny,)),
            dma((ny,)),
            dma((ny,)),
            dma((nz,)),
            dma((nz,)),
            dma((nz,)),
            dma((ny, 2)),
            dma((ny, 2)),
        ],
        compiler_params=pltpu.CompilerParams(
            vmem_limit_bytes=60 * 2**20, collective_id=0, has_side_effects=True
        ),
        name="newton_step",
    )(labels.reshape(1, rows), weights, features)


def solution(mesh, nx=4):
    dims = (mesh.shape["group"] // 2, mesh.shape["rows"] // nx, nx)
    return jax.shard_map(
        functools.partial(per_device, dims),
        mesh=mesh,
        in_specs=(P(("group", "rows"), None), P(("group", "rows")), P()),
        out_specs=P(None, ("group", "rows")),
        check_vma=False,
    )
```

```python
import functools

import jax
import jax.numpy as jnp
from jax import lax
from jax.experimental import pallas as pl
from jax.experimental.pallas import tpu as pltpu
from jax.sharding import PartitionSpec as P

RIDGE = 0.001
MESH = pl.DeviceIdType.MESH
NT = (((1,), (1,)), ((), ()))
F32 = jnp.float32
BF16 = jnp.bfloat16


def rows_product(left, data):
    return lax.dot_general(left, data, NT, preferred_element_type=F32)


def total_of(array):
    return jnp.sum(jnp.sum(array, axis=0, keepdims=True), axis=1, keepdims=True)


def fold(array):
    height, width = array.shape
    array = sum(array[k : k + 8] for k in range(0, height, 8))
    return sum(array[:, k : k + 128] for k in range(0, width, 128))


def near(n):
    return sorted(range(n), key=lambda k: min(k, n - k))


def kernel(
    dims,
    labels_hbm,
    w_hbm,
    f_hbm,
    out_ref,
    feat,
    feat_t,
    labels,
    wts,
    pair_src,
    pair,
    part,
    got,
    line_src,
    line,
    first,
    term,
    gotx,
    zsrc,
    gotz,
    sums,
    stat_src,
    stat_z,
    stat_y,
    load_sem,
    w_sem,
    label_sem,
    send,
    recv,
    pair_sem,
    first_sem,
    rsx_sem,
    agz_sem,
    agx_sem,
    bulk_sem,
    fwd_sem,
):
    ny, nz, nx = dims
    ng = 2 * ny
    classes, depth = wts.shape
    rows = feat.shape[0]
    plane = ny * nx
    half = depth // 2
    block = half // ny
    wide = block // nx
    zblock = depth // nz
    zwide = zblock // nx
    shard_rows = rows * nz * nx
    total_rows = shard_rows * ng
    near_y, near_z, near_x = near(ny), near(nz), near(nx)
    sides, across = near_y[1:3], near_y[3]

    g, r = lax.axis_index("group"), lax.axis_index("rows")
    y, c = g // 2, g % 2
    z, x = r // nx, r % nx
    slot = c * ny + y

    def cols(start, size):
        return pl.ds(pl.multiple_of(start, 128), size)

    def push(src, dst, ssem, rsem, yy, cc, zz, xx):
        pltpu.make_async_remote_copy(
            src_ref=src,
            dst_ref=dst,
            send_sem=ssem,
            recv_sem=rsem,
            device_id=(yy * 2 + cc, zz * nx + xx),
            device_id_type=MESH,
        ).start()

    def wait(ref, sem):
        pltpu.make_async_copy(ref, ref, sem).wait()

    w_copy = pltpu.make_async_copy(w_hbm, wts, w_sem)
    w_copy.start()
    label_copy = pltpu.make_async_copy(labels_hbm, labels, label_sem)
    label_copy.start()
    loads = []
    for k in range(ng):
        span = pl.ds(k * (depth // ng), depth // ng)
        loads.append(pltpu.make_async_copy(f_hbm.at[:, span], feat.at[:, span], load_sem.at[k]))
        loads[-1].start()
    barrier = pltpu.get_barrier_semaphore()
    others = [(j, k, i) for j in near_y[::-1] for k in near_x[::-1] for i in (1, 0) if (j, k, i) != (0, 0, 0)]
    others.sort(key=lambda o: -min(o[0], ny - o[0]) - min(o[1], nx - o[1]))
    for j, k, i in others:
        there = (((y + j) % ny) * 2 + (c + i) % 2, z * nx + (x + k) % nx)
        pl.semaphore_signal(barrier, 1, device_id=there, device_id_type=MESH)
    for k in near_z[:0:-1]:
        pl.semaphore_signal(barrier, 1, device_id=(g, ((z + k) % nz) * nx + x), device_id_type=MESH)

    def turn(begin, end):
        for k in range(begin, end):
            span = slice(k * block, (k + 1) * block)
            feat_t[span, :] = feat[:, span].T

    w_copy.wait()
    logits = jnp.zeros((classes, rows), F32)
    for k in range(ng):
        loads[k].wait()
        span = slice(k * (depth // ng), (k + 1) * (depth // ng))
        logits += rows_product(wts[:, span].astype(BF16), feat[:, span])
    e = jnp.exp(logits - jnp.max(logits, axis=0, keepdims=True))
    prob = e / jnp.sum(e, axis=0, keepdims=True)
    label_copy.wait()
    onehot = labels[...] == lax.broadcasted_iota(jnp.int32, (classes, rows), 0)
    resid = (prob - onehot.astype(F32)).astype(BF16)

    pl.semaphore_wait(barrier, len(others) + nz - 1)
    for j in near_y[::-1]:
        yy = (y + j) % ny
        span = cols((1 - c) * half + yy * block, block)
        pair_src[yy] = jnp.dot(resid, feat[:, span], preferred_element_type=F32)
        push(pair_src.at[yy], pair.at[yy], send.at[0], pair_sem.at[yy], y, 1 - c, z, x)
    for j in near_y[::-1]:
        yy = (y + j) % ny
        begin = c * half + yy * block
        mine = jnp.dot(resid, feat[:, cols(begin, block)], preferred_element_type=F32)
        wait(pair.at[yy], pair_sem.at[yy])
        part[:, cols(begin, block)] = (mine + pair[yy]).astype(BF16)
        for k in near_x[::-1]:
            xx = (x + k) % nx
            if j or k:
                there = part.at[:, cols(begin + xx * wide, wide)]
                push(there, got.at[y * nx + x], send.at[1], recv.at[0], yy, c, z, xx)
    own = cols(slot * block + x * wide, wide)
    got[y * nx + x] = part[:, own]
    turn(0, ng // 2)
    wait(got.at[pl.ds(0, plane - 1)], recv.at[0])
    share = jnp.zeros((classes, wide), F32)
    for k in range(plane):
        share += got[k].astype(F32)
    line_src[...] = share
    for k in near_z[:0:-1]:
        push(line_src, line.at[z], send.at[2], recv.at[1], y, c, (z + k) % nz, x)
    line[z] = line_src[...]
    turn(ng // 2, ng)
    wait(line.at[pl.ds(0, nz - 1)], recv.at[1])
    share = jnp.zeros((classes, wide), F32)
    for k in range(nz):
        share += line[k]
    first[:, own] = (-(share / total_rows + RIDGE * wts[:, own])).astype(BF16)
    for j, k, i in others:
        there = first.at[:, own]
        push(there, there, send.at[3], first_sem.at[slot], (y + j) % ny, (c + i) % 2, z, (x + k) % nx)

    u1 = jnp.zeros((classes, rows), F32)
    for j in near_y:
        for i in (0, 1):
            there = (c + i) % 2 * ny + (y + j) % ny
            span = cols(there * block, block)
            wait(got.at[pl.ds(0, nx if i or j else nx - 1)], first_sem.at[there])
            u1 += jnp.dot(first[:, span], feat_t[span, :], preferred_element_type=F32)
    c1 = (prob * (u1 - jnp.sum(prob * u1, axis=0, keepdims=True))).astype(BF16)

    for k in near_z[::-1]:
        zz = (z + k) % nz
        begin = zz * zblock
        term[:, cols(begin, zblock)] = jnp.dot(
            c1, feat[:, cols(begin, zblock)], preferred_element_type=F32
        ).astype(BF16)
        for i in near_x[:0:-1]:
            xx = (x + i) % nx
            push(term.at[:, cols(begin + xx * zwide, zwide)], gotx.at[zz, x], send.at[5], rsx_sem.at[zz], y, c, z, xx)
        gotx[zz, x] = term[:, cols(begin + x * zwide, zwide)]
    r0_r0 = jnp.zeros((8, 128), F32)
    for k in range(ng):
        r0 = first[:, k * block : (k + 1) * block].astype(F32)
        r0_r0 += fold(r0 * r0)
    rr0 = total_of(r0_r0)
    for k in near_z[::-1]:
        zz = (z + k) % nz
        wait(gotx.at[zz, pl.ds(0, nx - 1)], rsx_sem.at[zz])
        share = jnp.zeros((classes, zwide), F32)
        for i in range(nx):
            share += gotx[zz, i].astype(F32)
        if k:
            zsrc[zz] = share.astype(BF16)
            push(zsrc.at[zz], gotz.at[z], send.at[6], recv.at[2], y, c, zz, x)
        else:
            gotz[z] = share.astype(BF16)
    wait(gotz.at[pl.ds(0, nz - 1)], recv.at[2])
    share = jnp.zeros((classes, zwide), F32)
    for k in range(nz):
        share += gotz[k].astype(F32)

    own = cols(z * zblock + x * zwide, zwide)
    sums[slot, :, own] = share.astype(BF16)
    there = sums.at[slot, :, own]
    for k in near_z[:0:-1]:
        push(there, there, send.at[7], agz_sem.at[z], y, c, (z + k) % nz, x)
    for k in near_z:
        zz = (z + k) % nz
        there = sums.at[slot, :, cols(zz * zblock + x * zwide, zwide)]
        if k:
            wait(there, agz_sem.at[zz])
        for i in near_x[:0:-1]:
            push(there, there, send.at[8], agx_sem.at[zz], y, c, z, (x + i) % nx)

    w1 = jnp.zeros((classes, rows), F32)
    r0_s = jnp.zeros((8, 128), F32)
    for n, k in enumerate(near_z):
        zz = (z + k) % nz
        span = cols(zz * zblock, zblock)
        wait(gotx.at[0, pl.ds(0, nx - 1)], agx_sem.at[zz])
        for j in near_y[:0:-1]:
            there = sums.at[slot, :, span]
            push(there, there, send.at[9], bulk_sem.at[y, n // (nz // 2)], (y + j) % ny, c, z, x)
        w1 += jnp.dot(sums[slot, :, span], feat_t[span, :], preferred_element_type=F32)
        r0_s += fold(first[:, span].astype(F32) * sums[slot, :, span].astype(F32))

    c_u1 = prob * (u1 - jnp.sum(prob * u1, axis=0, keepdims=True))
    c_w1 = prob * (w1 - jnp.sum(prob * w1, axis=0, keepdims=True))
    row = lax.broadcasted_iota(jnp.int32, (8, 128), 0)
    three = [jnp.sum(fold(v), axis=0, keepdims=True) for v in (c_u1 * u1, c_u1 * w1, c_w1 * w1)]
    stat_src[0] = jnp.where(row == 0, three[0], jnp.where(row == 1, three[1], three[2]))
    for k in near_z[:0:-1]:
        push(stat_src.at[0], stat_z.at[z], send.at[10], recv.at[3], y, c, (z + k) % nz, x)
    stat_z[z] = stat_src[0]
    push(sums.at[slot], sums.at[slot], send.at[11], recv.at[4], y, 1 - c, z, x)

    alpha1 = rr0 / (total_of(r0_s) / shard_rows + RIDGE * rr0)
    keep, drop = 1.0 - alpha1 * RIDGE, alpha1 / shard_rows
    r1_r1 = jnp.zeros((8, 128), F32)
    for k in range(ng):
        span = slice(k * block, (k + 1) * block)
        r1 = keep * first[:, span].astype(F32) - drop * sums[slot, :, span].astype(F32)
        r1_r1 += fold(r1 * r1)
    rr1 = total_of(r1_r1)
    beta = rr1 / rr0
    pp = rr1 + beta * beta * rr0
    rest = jnp.where(row == 3, rr1, jnp.where(row == 4, pp, jnp.where(row == 5, alpha1, beta)))

    def pass_on(n):
        for j in near_y[1:]:
            yy = (y + j) % ny
            wait(sums.at[0, :, pl.ds(0, half)], bulk_sem.at[yy, n])
            for k in near_z[n * (nz // 2) : (n + 1) * (nz // 2)]:
                there = sums.at[c * ny + yy, :, cols(((z + k) % nz) * zblock, zblock)]
                push(there, there, send.at[12], fwd_sem.at[yy, n], y, 1 - c, z, x)

    def products(n):
        for j in near_y[1:]:
            wait(sums.at[0, :, pl.ds(0, half)], fwd_sem.at[(y + j) % ny, n])
        total = jnp.zeros((ng * classes, rows), F32)
        for k in near_z[n * (nz // 2) : (n + 1) * (nz // 2)]:
            span = cols(((z + k) % nz) * zblock, zblock)
            mine = sums[:, :, span].reshape(ng * classes, zblock)
            total += jnp.dot(mine, feat_t[span, :], preferred_element_type=F32)
        return total

    pass_on(0)
    wait(stat_z.at[pl.ds(0, nz - 1)], recv.at[3])
    curve = jnp.zeros((8, 128), F32)
    for k in range(nz):
        curve += stat_z[k]
    stat_src[1] = jnp.where(row < 3, curve, rest)
    for j, k, i in others:
        push(
            stat_src.at[1], stat_y.at[slot * nx + x], send.at[13], recv.at[5],
            (y + j) % ny, (c + i) % 2, z, (x + k) % nx,
        )
    stat_y[slot * nx + x] = stat_src[1]
    wait(sums.at[0], recv.at[4])
    w_all = products(0)
    pass_on(1)
    w_all += products(1)

    wait(stat_y.at[pl.ds(0, ng * nx - 1)], recv.at[5])
    scale = jnp.zeros((1, 1), F32)
    result = logits
    for there in range(ng):
        stats = stat_y[there * nx]
        for i in range(1, nx):
            stats = jnp.where(row < 3, stats + stat_y[there * nx + i], stats)
        uu, uw, ww = (jnp.sum(stats[i : i + 1], axis=1, keepdims=True) for i in range(3))
        rr, pp, alpha, beta = (stats[i : i + 1, 0:1] for i in range(3, 7))
        keep, drop = 1.0 + beta - RIDGE * alpha, alpha / shard_rows
        curve = keep * keep * uu - 2.0 * keep * drop * uw + drop * drop * ww
        alpha2 = rr / (curve / shard_rows + RIDGE * pp)
        scale += alpha + alpha2 * keep
        result -= (alpha2 * drop / ng) * w_all[there * classes : (there + 1) * classes]
    out_ref[...] = result + (scale / ng) * u1

    wait(pair_src, send.at[0])
    wait(got.at[pl.ds(0, plane - 1)], send.at[1])
    wait(line.at[pl.ds(0, nz - 1)], send.at[2])
    wait(first.at[:, pl.ds(0, depth - wide)], send.at[3])
    wait(gotx.at[:, pl.ds(0, nx - 1)], send.at[5])
    wait(gotz.at[pl.ds(0, nz - 1)], send.at[6])
    wait(gotz.at[pl.ds(0, nz - 1)], send.at[7])
    wait(gotx.at[:, pl.ds(0, nx - 1)], send.at[8])
    wait(sums.at[pl.ds(0, ny - 1)], send.at[9])
    wait(stat_z.at[pl.ds(0, nz - 1)], send.at[10])
    wait(sums.at[0], send.at[11])
    wait(sums.at[pl.ds(0, ny - 1)], send.at[12])
    wait(stat_y.at[pl.ds(0, ng * nx - 1)], send.at[13])


def per_device(dims, features, labels, weights):
    ny, nz, nx = dims
    ng = 2 * ny
    rows, depth = features.shape
    classes = weights.shape[0]
    block = depth // ng
    wide, zwide = block // nx, depth // (nz * nx)
    dma = pltpu.SemaphoreType.DMA
    any_space = pl.BlockSpec(memory_space=pl.ANY)
    return pl.pallas_call(
        functools.partial(kernel, dims),
        out_shape=pltpu.VMEM((classes, rows), F32),
        in_specs=[any_space] * 3,
        out_specs=pl.BlockSpec(memory_space=pltpu.VMEM),
        scratch_shapes=[
            pltpu.VMEM((rows, depth), BF16),
            pltpu.VMEM((depth, rows), BF16),
            pltpu.VMEM((1, rows), jnp.int32),
            pltpu.VMEM((classes, depth), F32),
            pltpu.VMEM((ny, classes, block), F32),
            pltpu.VMEM((ny, classes, block), F32),
            pltpu.VMEM((classes, depth), BF16),
            pltpu.VMEM((ny * nx, classes, wide), BF16),
            pltpu.VMEM((classes, wide), F32),
            pltpu.VMEM((nz, classes, wide), F32),
            pltpu.VMEM((classes, depth), BF16),
            pltpu.VMEM((classes, depth), BF16),
            pltpu.VMEM((nz, nx, classes, zwide), BF16),
            pltpu.VMEM((nz, classes, zwide), BF16),
            pltpu.VMEM((nz, classes, zwide), BF16),
            pltpu.VMEM((ng, classes, depth), BF16),
            pltpu.VMEM((2, 8, 128), F32),
            pltpu.VMEM((nz, 8, 128), F32),
            pltpu.VMEM((ng * nx, 8, 128), F32),
            dma((ng,)),
            dma,
            dma,
            dma((14,)),
            dma((6,)),
            dma((ny,)),
            dma((ng,)),
            dma((nz,)),
            dma((nz,)),
            dma((nz,)),
            dma((ny, 2)),
            dma((ny, 2)),
        ],
        compiler_params=pltpu.CompilerParams(
            vmem_limit_bytes=60 * 2**20, collective_id=0, has_side_effects=True
        ),
        name="newton_step",
    )(labels.reshape(1, rows), weights, features)


def solution(mesh, nx=4):
    dims = (mesh.shape["group"] // 2, mesh.shape["rows"] // nx, nx)
    return jax.shard_map(
        functools.partial(per_device, dims),
        mesh=mesh,
        in_specs=(P(("group", "rows"), None), P(("group", "rows")), P()),
        out_specs=P(None, ("group", "rows")),
        check_vma=False,
    )
```

```python
import functools

import jax
import jax.numpy as jnp
from jax import lax
from jax.experimental import pallas as pl
from jax.experimental.pallas import tpu as pltpu
from jax.sharding import PartitionSpec as P

RIDGE = 0.001
MESH = pl.DeviceIdType.MESH
NT = (((1,), (1,)), ((), ()))
F32 = jnp.float32
BF16 = jnp.bfloat16


def rows_product(left, data):
    return lax.dot_general(left, data, NT, preferred_element_type=F32)


def total_of(array):
    return jnp.sum(jnp.sum(array, axis=0, keepdims=True), axis=1, keepdims=True)


def fold(array):
    height, width = array.shape
    array = sum(array[k : k + 8] for k in range(0, height, 8))
    return sum(array[:, k : k + 128] for k in range(0, width, 128))


def near(n):
    return sorted(range(n), key=lambda k: min(k, n - k))


def kernel(
    dims,
    labels_hbm,
    w_hbm,
    f_hbm,
    out_ref,
    feat,
    feat_t,
    labels,
    wts,
    pair_src,
    pair,
    part,
    got,
    line_src,
    line,
    first,
    term,
    gotx,
    zsrc,
    gotz,
    sums,
    stat_src,
    stat_z,
    stat_y,
    load_sem,
    w_sem,
    label_sem,
    send,
    recv,
    pair_sem,
    first_sem,
    rsx_sem,
    agz_sem,
    agx_sem,
    bulk_sem,
    fwd_sem,
):
    ny, nz, nx = dims
    ng = 2 * ny
    classes, depth = wts.shape
    rows = feat.shape[0]
    plane = ny * nx
    half = depth // 2
    block = half // ny
    wide = block // nx
    zblock = depth // nz
    zwide = zblock // nx
    shard_rows = rows * nz * nx
    total_rows = shard_rows * ng
    near_y, near_z, near_x = near(ny), near(nz), near(nx)
    sides, across = near_y[1:3], near_y[3]

    g, r = lax.axis_index("group"), lax.axis_index("rows")
    y, c = g // 2, g % 2
    z, x = r // nx, r % nx
    slot = c * ny + y

    def cols(start, size):
        return pl.ds(pl.multiple_of(start, 128), size)

    def push(src, dst, ssem, rsem, yy, cc, zz, xx):
        pltpu.make_async_remote_copy(
            src_ref=src,
            dst_ref=dst,
            send_sem=ssem,
            recv_sem=rsem,
            device_id=(yy * 2 + cc, zz * nx + xx),
            device_id_type=MESH,
        ).start()

    def wait(ref, sem):
        pltpu.make_async_copy(ref, ref, sem).wait()

    w_copy = pltpu.make_async_copy(w_hbm, wts, w_sem)
    w_copy.start()
    label_copy = pltpu.make_async_copy(labels_hbm, labels, label_sem)
    label_copy.start()
    loads = []
    for k in range(ng):
        span = pl.ds(k * (depth // ng), depth // ng)
        loads.append(pltpu.make_async_copy(f_hbm.at[:, span], feat.at[:, span], load_sem.at[k]))
        loads[-1].start()
    barrier = pltpu.get_barrier_semaphore()
    others = [(j, k, i) for j in near_y[::-1] for k in near_x[::-1] for i in (1, 0) if (j, k, i) != (0, 0, 0)]
    others.sort(key=lambda o: -min(o[0], ny - o[0]) - min(o[1], nx - o[1]))
    for j, k, i in others:
        there = (((y + j) % ny) * 2 + (c + i) % 2, z * nx + (x + k) % nx)
        pl.semaphore_signal(barrier, 1, device_id=there, device_id_type=MESH)
    for k in near_z[:0:-1]:
        pl.semaphore_signal(barrier, 1, device_id=(g, ((z + k) % nz) * nx + x), device_id_type=MESH)

    def turn(begin, end):
        for k in range(begin, end):
            span = slice(k * block, (k + 1) * block)
            feat_t[span, :] = feat[:, span].T

    w_copy.wait()
    logits = jnp.zeros((classes, rows), F32)
    for k in range(ng):
        loads[k].wait()
        span = slice(k * (depth // ng), (k + 1) * (depth // ng))
        logits += rows_product(wts[:, span].astype(BF16), feat[:, span])
    e = jnp.exp(logits - jnp.max(logits, axis=0, keepdims=True))
    prob = e / jnp.sum(e, axis=0, keepdims=True)
    label_copy.wait()
    onehot = labels[...] == lax.broadcasted_iota(jnp.int32, (classes, rows), 0)
    resid = (prob - onehot.astype(F32)).astype(BF16)

    pl.semaphore_wait(barrier, len(others) + nz - 1)
    for j in near_y[::-1]:
        yy = (y + j) % ny
        span = cols((1 - c) * half + yy * block, block)
        pair_src[yy] = jnp.dot(resid, feat[:, span], preferred_element_type=F32)
        push(pair_src.at[yy], pair.at[yy], send.at[0], pair_sem.at[yy], y, 1 - c, z, x)
    for j in near_y[::-1]:
        yy = (y + j) % ny
        begin = c * half + yy * block
        mine = jnp.dot(resid, feat[:, cols(begin, block)], preferred_element_type=F32)
        wait(pair.at[yy], pair_sem.at[yy])
        part[:, cols(begin, block)] = (mine + pair[yy]).astype(BF16)
        for k in near_x[::-1]:
            xx = (x + k) % nx
            if j or k:
                there = part.at[:, cols(begin + xx * wide, wide)]
                push(there, got.at[y * nx + x], send.at[1], recv.at[0], yy, c, z, xx)
    own = cols(slot * block + x * wide, wide)
    got[y * nx + x] = part[:, own]
    turn(0, ng // 2)
    wait(got.at[pl.ds(0, plane - 1)], recv.at[0])
    share = jnp.zeros((classes, wide), F32)
    for k in range(plane):
        share += got[k].astype(F32)
    line_src[...] = share
    for k in near_z[:0:-1]:
        push(line_src, line.at[z], send.at[2], recv.at[1], y, c, (z + k) % nz, x)
    line[z] = line_src[...]
    turn(ng // 2, ng)
    wait(line.at[pl.ds(0, nz - 1)], recv.at[1])
    share = jnp.zeros((classes, wide), F32)
    for k in range(nz):
        share += line[k]
    first[:, own] = (-(share / total_rows + RIDGE * wts[:, own])).astype(BF16)
    for j, k, i in others:
        there = first.at[:, own]
        push(there, there, send.at[3], first_sem.at[slot], (y + j) % ny, (c + i) % 2, z, (x + k) % nx)

    u1 = jnp.zeros((classes, rows), F32)
    for j in near_y:
        for i in (0, 1):
            there = (c + i) % 2 * ny + (y + j) % ny
            span = cols(there * block, block)
            wait(got.at[pl.ds(0, nx if i or j else nx - 1)], first_sem.at[there])
            u1 += jnp.dot(first[:, span], feat_t[span, :], preferred_element_type=F32)
    c1 = (prob * (u1 - jnp.sum(prob * u1, axis=0, keepdims=True))).astype(BF16)

    for k in near_z[::-1]:
        zz = (z + k) % nz
        begin = zz * zblock
        term[:, cols(begin, zblock)] = jnp.dot(
            c1, feat[:, cols(begin, zblock)], preferred_element_type=F32
        ).astype(BF16)
        for i in near_x[:0:-1]:
            xx = (x + i) % nx
            push(term.at[:, cols(begin + xx * zwide, zwide)], gotx.at[zz, x], send.at[5], rsx_sem.at[zz], y, c, z, xx)
        gotx[zz, x] = term[:, cols(begin + x * zwide, zwide)]
    r0_r0 = jnp.zeros((8, 128), F32)
    for k in range(ng):
        r0 = first[:, k * block : (k + 1) * block].astype(F32)
        r0_r0 += fold(r0 * r0)
    rr0 = total_of(r0_r0)
    for k in near_z[::-1]:
        zz = (z + k) % nz
        wait(gotx.at[zz, pl.ds(0, nx - 1)], rsx_sem.at[zz])
        share = jnp.zeros((classes, zwide), F32)
        for i in range(nx):
            share += gotx[zz, i].astype(F32)
        if k:
            zsrc[zz] = share.astype(BF16)
            push(zsrc.at[zz], gotz.at[z], send.at[6], recv.at[2], y, c, zz, x)
        else:
            gotz[z] = share.astype(BF16)
    wait(gotz.at[pl.ds(0, nz - 1)], recv.at[2])
    share = jnp.zeros((classes, zwide), F32)
    for k in range(nz):
        share += gotz[k].astype(F32)

    own = cols(z * zblock + x * zwide, zwide)
    sums[slot, :, own] = share.astype(BF16)
    there = sums.at[slot, :, own]
    for k in near_z[:0:-1]:
        push(there, there, send.at[7], agz_sem.at[z], y, c, (z + k) % nz, x)
    for k in near_z:
        zz = (z + k) % nz
        there = sums.at[slot, :, cols(zz * zblock + x * zwide, zwide)]
        if k:
            wait(there, agz_sem.at[zz])
        for i in near_x[:0:-1]:
            push(there, there, send.at[8], agx_sem.at[zz], y, c, z, (x + i) % nx)
        push(there, there, send.at[14], recv.at[6], (y + across) % ny, c, z, x)

    w1 = jnp.zeros((classes, rows), F32)
    r0_s = jnp.zeros((8, 128), F32)
    for n, k in enumerate(near_z):
        zz = (z + k) % nz
        span = cols(zz * zblock, zblock)
        wait(gotx.at[0, pl.ds(0, nx - 1)], agx_sem.at[zz])
        for j in sides:
            there = sums.at[slot, :, span]
            push(there, there, send.at[9], bulk_sem.at[y, n // (nz // 2)], (y + j) % ny, c, z, x)
        w1 += jnp.dot(sums[slot, :, span], feat_t[span, :], preferred_element_type=F32)
        r0_s += fold(first[:, span].astype(F32) * sums[slot, :, span].astype(F32))

    c_u1 = prob * (u1 - jnp.sum(prob * u1, axis=0, keepdims=True))
    c_w1 = prob * (w1 - jnp.sum(prob * w1, axis=0, keepdims=True))
    row = lax.broadcasted_iota(jnp.int32, (8, 128), 0)
    three = [jnp.sum(fold(v), axis=0, keepdims=True) for v in (c_u1 * u1, c_u1 * w1, c_w1 * w1)]
    stat_src[0] = jnp.where(row == 0, three[0], jnp.where(row == 1, three[1], three[2]))
    for k in near_z[:0:-1]:
        push(stat_src.at[0], stat_z.at[z], send.at[10], recv.at[3], y, c, (z + k) % nz, x)
    stat_z[z] = stat_src[0]
    push(sums.at[slot], sums.at[slot], send.at[11], recv.at[4], y, 1 - c, z, x)

    alpha1 = rr0 / (total_of(r0_s) / shard_rows + RIDGE * rr0)
    keep, drop = 1.0 - alpha1 * RIDGE, alpha1 / shard_rows
    r1_r1 = jnp.zeros((8, 128), F32)
    for k in range(ng):
        span = slice(k * block, (k + 1) * block)
        r1 = keep * first[:, span].astype(F32) - drop * sums[slot, :, span].astype(F32)
        r1_r1 += fold(r1 * r1)
    rr1 = total_of(r1_r1)
    beta = rr1 / rr0
    pp = rr1 + beta * beta * rr0
    rest = jnp.where(row == 3, rr1, jnp.where(row == 4, pp, jnp.where(row == 5, alpha1, beta)))

    def parts(n):
        return [cols(((z + k) % nz) * zblock, zblock) for k in near_z[n * (nz // 2) : (n + 1) * (nz // 2)]]

    def hand_over(yy, n):
        for span in parts(n):
            there = sums.at[c * ny + yy, :, span]
            push(there, there, send.at[12], fwd_sem.at[yy, n], y, 1 - c, z, x)

    def pass_on(n):
        for j in sides:
            yy = (y + j) % ny
            wait(sums.at[0, :, pl.ds(0, half)], bulk_sem.at[yy, n])
            hand_over(yy, n)

    far_y = (y + across) % ny

    def share_across():
        wait(gotz, recv.at[6])
        for zz in range(nz):
            there = sums.at[c * ny + far_y, :, cols(zz * zblock + x * zwide, zwide)]
            for i in near_x[:0:-1]:
                push(there, there, send.at[4], recv.at[7], y, c, z, (x + i) % nx)

    def finish_across():
        wait(gotx.at[:, pl.ds(0, nx - 1)], recv.at[7])
        hand_over(far_y, 0)
        hand_over(far_y, 1)

    def products(n):
        for j in near_y[1:]:
            wait(sums.at[0, :, pl.ds(0, half)], fwd_sem.at[(y + j) % ny, n])
        total = jnp.zeros((ng * classes, rows), F32)
        for span in parts(n):
            mine = sums[:, :, span].reshape(ng * classes, zblock)
            total += jnp.dot(mine, feat_t[span, :], preferred_element_type=F32)
        return total

    share_across()
    pass_on(0)
    wait(stat_z.at[pl.ds(0, nz - 1)], recv.at[3])
    curve = jnp.zeros((8, 128), F32)
    for k in range(nz):
        curve += stat_z[k]
    stat_src[1] = jnp.where(row < 3, curve, rest)
    for j, k, i in others:
        push(
            stat_src.at[1], stat_y.at[slot * nx + x], send.at[13], recv.at[5],
            (y + j) % ny, (c + i) % 2, z, (x + k) % nx,
        )
    stat_y[slot * nx + x] = stat_src[1]
    wait(sums.at[0], recv.at[4])
    finish_across()
    pass_on(1)
    w_all = products(0)
    w_all += products(1)

    wait(stat_y.at[pl.ds(0, ng * nx - 1)], recv.at[5])
    scale = jnp.zeros((1, 1), F32)
    result = logits
    for there in range(ng):
        stats = stat_y[there * nx]
        for i in range(1, nx):
            stats = jnp.where(row < 3, stats + stat_y[there * nx + i], stats)
        uu, uw, ww = (jnp.sum(stats[i : i + 1], axis=1, keepdims=True) for i in range(3))
        rr, pp, alpha, beta = (stats[i : i + 1, 0:1] for i in range(3, 7))
        keep, drop = 1.0 + beta - RIDGE * alpha, alpha / shard_rows
        curve = keep * keep * uu - 2.0 * keep * drop * uw + drop * drop * ww
        alpha2 = rr / (curve / shard_rows + RIDGE * pp)
        scale += alpha + alpha2 * keep
        result -= (alpha2 * drop / ng) * w_all[there * classes : (there + 1) * classes]
    out_ref[...] = result + (scale / ng) * u1

    wait(pair_src, send.at[0])
    wait(got.at[pl.ds(0, plane - 1)], send.at[1])
    wait(line.at[pl.ds(0, nz - 1)], send.at[2])
    wait(first.at[:, pl.ds(0, depth - wide)], send.at[3])
    wait(gotx.at[:, pl.ds(0, nx - 1)], send.at[5])
    wait(gotz.at[pl.ds(0, nz - 1)], send.at[6])
    wait(gotz.at[pl.ds(0, nz - 1)], send.at[7])
    wait(gotx.at[:, pl.ds(0, nx - 1)], send.at[8])
    wait(gotx.at[:, pl.ds(0, nx - 1)], send.at[4])
    wait(sums.at[pl.ds(0, 2)], send.at[9])
    wait(gotz, send.at[14])
    wait(stat_z.at[pl.ds(0, nz - 1)], send.at[10])
    wait(sums.at[0], send.at[11])
    wait(sums.at[pl.ds(0, ny - 1)], send.at[12])
    wait(stat_y.at[pl.ds(0, ng * nx - 1)], send.at[13])


def per_device(dims, features, labels, weights):
    ny, nz, nx = dims
    ng = 2 * ny
    rows, depth = features.shape
    classes = weights.shape[0]
    block = depth // ng
    wide, zwide = block // nx, depth // (nz * nx)
    dma = pltpu.SemaphoreType.DMA
    any_space = pl.BlockSpec(memory_space=pl.ANY)
    return pl.pallas_call(
        functools.partial(kernel, dims),
        out_shape=pltpu.VMEM((classes, rows), F32),
        in_specs=[any_space] * 3,
        out_specs=pl.BlockSpec(memory_space=pltpu.VMEM),
        scratch_shapes=[
            pltpu.VMEM((rows, depth), BF16),
            pltpu.VMEM((depth, rows), BF16),
            pltpu.VMEM((1, rows), jnp.int32),
            pltpu.VMEM((classes, depth), F32),
            pltpu.VMEM((ny, classes, block), F32),
            pltpu.VMEM((ny, classes, block), F32),
            pltpu.VMEM((classes, depth), BF16),
            pltpu.VMEM((ny * nx, classes, wide), BF16),
            pltpu.VMEM((classes, wide), F32),
            pltpu.VMEM((nz, classes, wide), F32),
            pltpu.VMEM((classes, depth), BF16),
            pltpu.VMEM((classes, depth), BF16),
            pltpu.VMEM((nz, nx, classes, zwide), BF16),
            pltpu.VMEM((nz, classes, zwide), BF16),
            pltpu.VMEM((nz, classes, zwide), BF16),
            pltpu.VMEM((ng, classes, depth), BF16),
            pltpu.VMEM((2, 8, 128), F32),
            pltpu.VMEM((nz, 8, 128), F32),
            pltpu.VMEM((ng * nx, 8, 128), F32),
            dma((ng,)),
            dma,
            dma,
            dma((15,)),
            dma((8,)),
            dma((ny,)),
            dma((ng,)),
            dma((nz,)),
            dma((nz,)),
            dma((nz,)),
            dma((ny, 2)),
            dma((ny, 2)),
        ],
        compiler_params=pltpu.CompilerParams(
            vmem_limit_bytes=60 * 2**20, collective_id=0, has_side_effects=True
        ),
        name="newton_step",
    )(labels.reshape(1, rows), weights, features)


def solution(mesh, nx=4):
    dims = (mesh.shape["group"] // 2, mesh.shape["rows"] // nx, nx)
    return jax.shard_map(
        functools.partial(per_device, dims),
        mesh=mesh,
        in_specs=(P(("group", "rows"), None), P(("group", "rows")), P()),
        out_specs=P(None, ("group", "rows")),
        check_vma=False,
    )
```

```python
import functools

import jax
import jax.numpy as jnp
from jax import lax
from jax.experimental import pallas as pl
from jax.experimental.pallas import tpu as pltpu
from jax.sharding import PartitionSpec as P

RIDGE = 0.001
MESH = pl.DeviceIdType.MESH
NT = (((1,), (1,)), ((), ()))
F32 = jnp.float32
BF16 = jnp.bfloat16


def rows_product(left, data):
    return lax.dot_general(left, data, NT, preferred_element_type=F32)


def total_of(array):
    return jnp.sum(jnp.sum(array, axis=0, keepdims=True), axis=1, keepdims=True)


def fold(array):
    height, width = array.shape
    array = sum(array[k : k + 8] for k in range(0, height, 8))
    return sum(array[:, k : k + 128] for k in range(0, width, 128))


def near(n):
    return sorted(range(n), key=lambda k: min(k, n - k))


def kernel(
    dims,
    labels_hbm,
    w_hbm,
    f_hbm,
    out_ref,
    feat,
    feat_t,
    labels,
    wts,
    pair_src,
    pair,
    part,
    got,
    line_src,
    line,
    first,
    term,
    gotx,
    zsrc,
    gotz,
    sums,
    stat_src,
    stat_z,
    stat_y,
    load_sem,
    w_sem,
    label_sem,
    send,
    recv,
    pair_sem,
    first_sem,
    rsx_sem,
    agz_sem,
    agx_sem,
    bulk_sem,
    fwd_sem,
):
    ny, nz, nx = dims
    ng = 2 * ny
    classes, depth = wts.shape
    rows = feat.shape[0]
    plane = ny * nx
    half = depth // 2
    block = half // ny
    wide = block // nx
    zblock = depth // nz
    zwide = zblock // nx
    shard_rows = rows * nz * nx
    total_rows = shard_rows * ng
    near_y, near_z, near_x = near(ny), near(nz), near(nx)
    sides, across = near_y[1:3], near_y[3]

    g, r = lax.axis_index("group"), lax.axis_index("rows")
    y, c = g // 2, g % 2
    z, x = r // nx, r % nx
    slot = c * ny + y

    def cols(start, size):
        return pl.ds(pl.multiple_of(start, 128), size)

    def push(src, dst, ssem, rsem, yy, cc, zz, xx):
        pltpu.make_async_remote_copy(
            src_ref=src,
            dst_ref=dst,
            send_sem=ssem,
            recv_sem=rsem,
            device_id=(yy * 2 + cc, zz * nx + xx),
            device_id_type=MESH,
        ).start()

    def wait(ref, sem):
        pltpu.make_async_copy(ref, ref, sem).wait()

    w_copy = pltpu.make_async_copy(w_hbm, wts, w_sem)
    w_copy.start()
    label_copy = pltpu.make_async_copy(labels_hbm, labels, label_sem)
    label_copy.start()
    loads = []
    for k in range(ng // 2):
        span = pl.ds(k * 2 * block, 2 * block)
        loads.append(pltpu.make_async_copy(f_hbm.at[:, span], feat.at[:, span], load_sem.at[k]))
        loads[-1].start()
    barrier = pltpu.get_barrier_semaphore()
    others = [(j, k, i) for j in near_y[::-1] for k in near_x[::-1] for i in (1, 0) if (j, k, i) != (0, 0, 0)]
    others.sort(key=lambda o: -min(o[0], ny - o[0]) - min(o[1], nx - o[1]))
    for j, k, i in others:
        there = (((y + j) % ny) * 2 + (c + i) % 2, z * nx + (x + k) % nx)
        pl.semaphore_signal(barrier, 1, device_id=there, device_id_type=MESH)
    for k in near_z[:0:-1]:
        pl.semaphore_signal(barrier, 1, device_id=(g, ((z + k) % nz) * nx + x), device_id_type=MESH)

    def turn(begin, end):
        for k in range(begin, end):
            span = slice(k * block, (k + 1) * block)
            feat_t[span, :] = feat[:, span].T

    w_copy.wait()
    logits = jnp.zeros((classes, rows), F32)
    for k in range(ng // 2):
        loads[k].wait()
        span = slice(k * 2 * block, (k + 1) * 2 * block)
        logits += rows_product(wts[:, span].astype(BF16), feat[:, span])
    e = jnp.exp(logits - jnp.max(logits, axis=0, keepdims=True))
    prob = e / jnp.sum(e, axis=0, keepdims=True)
    label_copy.wait()
    onehot = labels[...] == lax.broadcasted_iota(jnp.int32, (classes, rows), 0)
    resid = (prob - onehot.astype(F32)).astype(BF16)

    pl.semaphore_wait(barrier, len(others) + nz - 1)
    for j in near_y[::-1]:
        yy = (y + j) % ny
        span = cols((1 - c) * half + yy * block, block)
        pair_src[yy] = jnp.dot(resid, feat[:, span], preferred_element_type=F32)
        push(pair_src.at[yy], pair.at[yy], send.at[0], pair_sem.at[yy], y, 1 - c, z, x)
    for j in near_y[::-1]:
        yy = (y + j) % ny
        begin = c * half + yy * block
        mine = jnp.dot(resid, feat[:, cols(begin, block)], preferred_element_type=F32)
        wait(pair.at[yy], pair_sem.at[yy])
        part[:, cols(begin, block)] = (mine + pair[yy]).astype(BF16)
        for k in near_x[::-1]:
            xx = (x + k) % nx
            if j or k:
                there = part.at[:, cols(begin + xx * wide, wide)]
                push(there, got.at[y * nx + x], send.at[1], recv.at[0], yy, c, z, xx)
    own = cols(slot * block + x * wide, wide)
    got[y * nx + x] = part[:, own]
    turn(0, ng // 2)
    wait(got.at[pl.ds(0, plane - 1)], recv.at[0])
    share = jnp.zeros((classes, wide), F32)
    for k in range(plane):
        share += got[k].astype(F32)
    line_src[...] = share
    for k in near_z[:0:-1]:
        push(line_src, line.at[z], send.at[2], recv.at[1], y, c, (z + k) % nz, x)
    line[z] = line_src[...]
    turn(ng // 2, ng)
    wait(line.at[pl.ds(0, nz - 1)], recv.at[1])
    share = jnp.zeros((classes, wide), F32)
    for k in range(nz):
        share += line[k]
    first[:, own] = (-(share / total_rows + RIDGE * wts[:, own])).astype(BF16)
    for j, k, i in others:
        there = first.at[:, own]
        push(there, there, send.at[3], first_sem.at[slot], (y + j) % ny, (c + i) % 2, z, (x + k) % nx)

    u1 = jnp.zeros((classes, rows), F32)
    for j in near_y:
        for i in (0, 1):
            there = (c + i) % 2 * ny + (y + j) % ny
            span = cols(there * block, block)
            wait(got.at[pl.ds(0, nx if i or j else nx - 1)], first_sem.at[there])
            u1 += jnp.dot(first[:, span], feat_t[span, :], preferred_element_type=F32)
    c1 = (prob * (u1 - jnp.sum(prob * u1, axis=0, keepdims=True))).astype(BF16)

    for k in near_z[::-1]:
        zz = (z + k) % nz
        begin = zz * zblock
        term[:, cols(begin, zblock)] = jnp.dot(
            c1, feat[:, cols(begin, zblock)], preferred_element_type=F32
        ).astype(BF16)
        for i in near_x[:0:-1]:
            xx = (x + i) % nx
            push(term.at[:, cols(begin + xx * zwide, zwide)], gotx.at[zz, x], send.at[5], rsx_sem.at[zz], y, c, z, xx)
        gotx[zz, x] = term[:, cols(begin + x * zwide, zwide)]
    r0_r0 = jnp.zeros((8, 128), F32)
    for k in range(ng):
        r0 = first[:, k * block : (k + 1) * block].astype(F32)
        r0_r0 += fold(r0 * r0)
    rr0 = total_of(r0_r0)
    for k in near_z[::-1]:
        zz = (z + k) % nz
        wait(gotx.at[zz, pl.ds(0, nx - 1)], rsx_sem.at[zz])
        share = jnp.zeros((classes, zwide), F32)
        for i in range(nx):
            share += gotx[zz, i].astype(F32)
        if k:
            zsrc[zz] = share.astype(BF16)
            push(zsrc.at[zz], gotz.at[z], send.at[6], recv.at[2], y, c, zz, x)
        else:
            gotz[z] = share.astype(BF16)
    wait(gotz.at[pl.ds(0, nz - 1)], recv.at[2])
    share = jnp.zeros((classes, zwide), F32)
    for k in range(nz):
        share += gotz[k].astype(F32)

    own = cols(z * zblock + x * zwide, zwide)
    sums[slot, :, own] = share.astype(BF16)
    there = sums.at[slot, :, own]
    for k in near_z[:0:-1]:
        push(there, there, send.at[7], agz_sem.at[z], y, c, (z + k) % nz, x)
    for k in near_z:
        zz = (z + k) % nz
        there = sums.at[slot, :, cols(zz * zblock + x * zwide, zwide)]
        if k:
            wait(there, agz_sem.at[zz])
        for i in near_x[:0:-1]:
            push(there, there, send.at[8], agx_sem.at[zz], y, c, z, (x + i) % nx)
        push(there, there, send.at[14], recv.at[6], (y + across) % ny, c, z, x)

    w1 = jnp.zeros((classes, rows), F32)
    r0_s = jnp.zeros((8, 128), F32)
    for n, k in enumerate(near_z):
        zz = (z + k) % nz
        span = cols(zz * zblock, zblock)
        wait(gotx.at[0, pl.ds(0, nx - 1)], agx_sem.at[zz])
        for j in sides:
            there = sums.at[slot, :, span]
            push(there, there, send.at[9], bulk_sem.at[y, n // (nz // 2)], (y + j) % ny, c, z, x)
        w1 += jnp.dot(sums[slot, :, span], feat_t[span, :], preferred_element_type=F32)
        r0_s += fold(first[:, span].astype(F32) * sums[slot, :, span].astype(F32))

    c_u1 = prob * (u1 - jnp.sum(prob * u1, axis=0, keepdims=True))
    c_w1 = prob * (w1 - jnp.sum(prob * w1, axis=0, keepdims=True))
    row = lax.broadcasted_iota(jnp.int32, (8, 128), 0)
    three = [jnp.sum(fold(v), axis=0, keepdims=True) for v in (c_u1 * u1, c_u1 * w1, c_w1 * w1)]
    stat_src[0] = jnp.where(row == 0, three[0], jnp.where(row == 1, three[1], three[2]))
    for k in near_z[:0:-1]:
        push(stat_src.at[0], stat_z.at[z], send.at[10], recv.at[3], y, c, (z + k) % nz, x)
    stat_z[z] = stat_src[0]
    push(sums.at[slot], sums.at[slot], send.at[11], recv.at[4], y, 1 - c, z, x)

    alpha1 = rr0 / (total_of(r0_s) / shard_rows + RIDGE * rr0)
    keep, drop = 1.0 - alpha1 * RIDGE, alpha1 / shard_rows
    r1_r1 = jnp.zeros((8, 128), F32)
    for k in range(ng):
        span = slice(k * block, (k + 1) * block)
        r1 = keep * first[:, span].astype(F32) - drop * sums[slot, :, span].astype(F32)
        r1_r1 += fold(r1 * r1)
    rr1 = total_of(r1_r1)
    beta = rr1 / rr0
    pp = rr1 + beta * beta * rr0
    rest = jnp.where(row == 3, rr1, jnp.where(row == 4, pp, jnp.where(row == 5, alpha1, beta)))

    def parts(n):
        return [cols(((z + k) % nz) * zblock, zblock) for k in near_z[n * (nz // 2) : (n + 1) * (nz // 2)]]

    def hand_over(yy, n):
        for span in parts(n):
            there = sums.at[c * ny + yy, :, span]
            push(there, there, send.at[12], fwd_sem.at[yy, n], y, 1 - c, z, x)

    def pass_on(n):
        for j in sides:
            yy = (y + j) % ny
            wait(sums.at[0, :, pl.ds(0, half)], bulk_sem.at[yy, n])
            hand_over(yy, n)

    far_y = (y + across) % ny

    def share_across():
        wait(gotz, recv.at[6])
        for zz in range(nz):
            there = sums.at[c * ny + far_y, :, cols(zz * zblock + x * zwide, zwide)]
            for i in near_x[:0:-1]:
                push(there, there, send.at[4], recv.at[7], y, c, z, (x + i) % nx)

    def finish_across():
        wait(gotx.at[:, pl.ds(0, nx - 1)], recv.at[7])
        hand_over(far_y, 0)
        hand_over(far_y, 1)

    def products(n):
        for j in near_y[1:]:
            wait(sums.at[0, :, pl.ds(0, half)], fwd_sem.at[(y + j) % ny, n])
        total = jnp.zeros((ng * classes, rows), F32)
        for span in parts(n):
            mine = sums[:, :, span].reshape(ng * classes, zblock)
            total += jnp.dot(mine, feat_t[span, :], preferred_element_type=F32)
        return total

    share_across()
    pass_on(0)
    wait(stat_z.at[pl.ds(0, nz - 1)], recv.at[3])
    curve = jnp.zeros((8, 128), F32)
    for k in range(nz):
        curve += stat_z[k]
    stat_src[1] = jnp.where(row < 3, curve, rest)
    for j, k, i in others:
        push(
            stat_src.at[1], stat_y.at[slot * nx + x], send.at[13], recv.at[5],
            (y + j) % ny, (c + i) % 2, z, (x + k) % nx,
        )
    stat_y[slot * nx + x] = stat_src[1]
    wait(sums.at[0], recv.at[4])
    finish_across()
    pass_on(1)
    w_all = products(0)
    w_all += products(1)

    wait(stat_y.at[pl.ds(0, ng * nx - 1)], recv.at[5])
    scale = jnp.zeros((1, 1), F32)
    result = logits
    for there in range(ng):
        stats = stat_y[there * nx]
        for i in range(1, nx):
            stats = jnp.where(row < 3, stats + stat_y[there * nx + i], stats)
        uu, uw, ww = (jnp.sum(stats[i : i + 1], axis=1, keepdims=True) for i in range(3))
        rr, pp, alpha, beta = (stats[i : i + 1, 0:1] for i in range(3, 7))
        keep, drop = 1.0 + beta - RIDGE * alpha, alpha / shard_rows
        curve = keep * keep * uu - 2.0 * keep * drop * uw + drop * drop * ww
        alpha2 = rr / (curve / shard_rows + RIDGE * pp)
        scale += alpha + alpha2 * keep
        result -= (alpha2 * drop / ng) * w_all[there * classes : (there + 1) * classes]
    out_ref[...] = result + (scale / ng) * u1

    wait(pair_src, send.at[0])
    wait(got.at[pl.ds(0, plane - 1)], send.at[1])
    wait(line.at[pl.ds(0, nz - 1)], send.at[2])
    wait(first.at[:, pl.ds(0, depth - wide)], send.at[3])
    wait(gotx.at[:, pl.ds(0, nx - 1)], send.at[5])
    wait(gotz.at[pl.ds(0, nz - 1)], send.at[6])
    wait(gotz.at[pl.ds(0, nz - 1)], send.at[7])
    wait(gotx.at[:, pl.ds(0, nx - 1)], send.at[8])
    wait(gotx.at[:, pl.ds(0, nx - 1)], send.at[4])
    wait(sums.at[pl.ds(0, 2)], send.at[9])
    wait(gotz, send.at[14])
    wait(stat_z.at[pl.ds(0, nz - 1)], send.at[10])
    wait(sums.at[0], send.at[11])
    wait(sums.at[pl.ds(0, ny - 1)], send.at[12])
    wait(stat_y.at[pl.ds(0, ng * nx - 1)], send.at[13])


def per_device(dims, features, labels, weights):
    ny, nz, nx = dims
    ng = 2 * ny
    rows, depth = features.shape
    classes = weights.shape[0]
    block = depth // ng
    wide, zwide = block // nx, depth // (nz * nx)
    dma = pltpu.SemaphoreType.DMA
    any_space = pl.BlockSpec(memory_space=pl.ANY)
    return pl.pallas_call(
        functools.partial(kernel, dims),
        out_shape=pltpu.VMEM((classes, rows), F32),
        in_specs=[any_space] * 3,
        out_specs=pl.BlockSpec(memory_space=pltpu.VMEM),
        scratch_shapes=[
            pltpu.VMEM((rows, depth), BF16),
            pltpu.VMEM((depth, rows), BF16),
            pltpu.VMEM((1, rows), jnp.int32),
            pltpu.VMEM((classes, depth), F32),
            pltpu.VMEM((ny, classes, block), F32),
            pltpu.VMEM((ny, classes, block), F32),
            pltpu.VMEM((classes, depth), BF16),
            pltpu.VMEM((ny * nx, classes, wide), BF16),
            pltpu.VMEM((classes, wide), F32),
            pltpu.VMEM((nz, classes, wide), F32),
            pltpu.VMEM((classes, depth), BF16),
            pltpu.VMEM((classes, depth), BF16),
            pltpu.VMEM((nz, nx, classes, zwide), BF16),
            pltpu.VMEM((nz, classes, zwide), BF16),
            pltpu.VMEM((nz, classes, zwide), BF16),
            pltpu.VMEM((ng, classes, depth), BF16),
            pltpu.VMEM((2, 8, 128), F32),
            pltpu.VMEM((nz, 8, 128), F32),
            pltpu.VMEM((ng * nx, 8, 128), F32),
            dma((ng // 2,)),
            dma,
            dma,
            dma((15,)),
            dma((8,)),
            dma((ny,)),
            dma((ng,)),
            dma((nz,)),
            dma((nz,)),
            dma((nz,)),
            dma((ny, 2)),
            dma((ny, 2)),
        ],
        compiler_params=pltpu.CompilerParams(
            vmem_limit_bytes=60 * 2**20, collective_id=0, has_side_effects=True
        ),
        name="newton_step",
    )(labels.reshape(1, rows), weights, features)


def solution(mesh, nx=4):
    dims = (mesh.shape["group"] // 2, mesh.shape["rows"] // nx, nx)
    return jax.shard_map(
        functools.partial(per_device, dims),
        mesh=mesh,
        in_specs=(P(("group", "rows"), None), P(("group", "rows")), P()),
        out_specs=P(None, ("group", "rows")),
        check_vma=False,
    )
```
